32 devices in a mesh: rows: 8 (over z, y), tgt: 4 (over x, core).
Axes of the slice: x: 2, y: 2, z: 4, core: 2. Of those that a mesh axis runs over, the one named last changes fastest.
Arguments:
- frames: bfloat16 [16384, 512], P('rows', 'tgt'), may hold values from -6 to 6
- weights: bfloat16 [512, 1024], replicated, may hold values from -0.25 to 0.25
- phases: float32 [1024], replicated, may hold values from -3.140625 to 3.140625
- residual: float32 [16384, 1024], P('rows', 'tgt'), may hold values from -6 to 6
Outputs:
- residual_next: float32 [16384, 1024], P('rows', 'tgt')
- coefficients: float32 [1024, 1024], P(None, 'tgt')
The draws below stay inside these ranges and needn't reach their ends.
All inputs are finite; a program needn't handle non-finite values.
Results may differ from the reference program's by a relative error of at most 0.0003.
Values may be sent and summed in bfloat16 or wider, within the bound.
A program may use at most 128 MiB of HBM per device.

```python
import jax
import jax.numpy as jnp
from jax import lax

DIN = 512
FEAT = 1024
TGT = 1024
TOTAL = 16384


def block_levels(own_key, extent, shards, smallest, top_value):
    def one(axis_at, blocks):
        steps = jax.random.uniform(jax.random.fold_in(jax.random.fold_in(own_key, 6), axis_at), (blocks,), jnp.float32, smallest / len(shards), top_value / len(shards))
        return jnp.repeat(jnp.exp(steps), extent[axis_at] // blocks).reshape((-1,) + (1,) * (len(extent) - axis_at - 1))

    level = one(*shards[0])
    for cut in shards[1:]:
        level = level * one(*cut)
    return level


def noise(rng, dims, spread, most, split=(), kind=jnp.bfloat16):
    result = jax.random.normal(rng, dims, jnp.float32) * spread
    if len(split) > 0:
        result = block_levels(rng, dims, split, -0.22, 0.18) * result
    return jnp.clip(result, min=-most, max=most).astype(kind)


def setup_inputs(seed: int = 0) -> dict:
    arg_keys = jax.random.split(jax.random.key(seed), 5)
    return {
        "frames": noise(arg_keys[0], (TOTAL, DIN), 1.0, 6.0, ((0, 8), (1, 4))),
        "weights": noise(arg_keys[1], (DIN, FEAT), DIN ** -0.5, 0.25),
        "phases": jnp.clip(jax.random.uniform(arg_keys[2], (FEAT,), jnp.float32, -3.140625, 3.140625), -3.140625, 3.140625),
        "residual": noise(arg_keys[3], (TOTAL, TGT), 1.0, 6.0, ((0, 8), (1, 4)), jnp.float32),
    }


def reference(frames, weights, phases, residual):
    highest = lax.Precision.HIGHEST
    preact = jnp.dot(frames.astype(jnp.float32), weights.astype(jnp.float32), preferred_element_type=jnp.float32)
    feature = jnp.sqrt(2.0 / FEAT) * jnp.cos(preact + phases[None, :])
    gram_matrix = jnp.dot(feature.T.astype(jnp.float32), feature.astype(jnp.float32), precision=highest, preferred_element_type=jnp.float32)
    gram_matrix = gram_matrix + 0.1 * TOTAL / FEAT * jnp.eye(FEAT, dtype=jnp.float32)
    correlation = jnp.dot(feature.T.astype(jnp.float32), residual.astype(jnp.float32), precision=highest, preferred_element_type=jnp.float32)
    factor = jnp.linalg.cholesky(gram_matrix)
    coefficients = jax.scipy.linalg.cho_solve((factor, True), correlation)
    residual_next = residual - jnp.dot(feature.astype(jnp.float32), coefficients.astype(jnp.float32), precision=highest, preferred_element_type=jnp.float32)
    return (residual_next, coefficients)
```

```python
import functools
import math

import jax
import jax.numpy as jnp
from jax import lax
from jax.experimental import pallas as pl
from jax.experimental.pallas import tpu as pltpu
from jax.sharding import PartitionSpec as P

HIGHEST = lax.Precision.HIGHEST
PANEL = 128
LIMIT = 48 * 1024 * 1024
HALF = (
    0.9999999997778334,
    -0.49999999352232993 / 4,
    0.04166663603866973 / 16,
    -0.001388835871629621 / 64,
    2.4760028045058155e-05 / 256,
    -2.604918848612031e-07 / 1024,
)


def cosine(angle):
    turns = jnp.round(angle * (1.0 / (2.0 * math.pi)))
    rest = (angle - turns * 6.28125) - turns * (2.0 * math.pi - 6.28125)
    square = rest * rest
    half = jnp.full_like(square, HALF[-1])
    for term in HALF[-2::-1]:
        half = half * square + term
    return 2.0 * half * half - 1.0


def dot(a, b):
    return jnp.dot(a, b, precision=HIGHEST, preferred_element_type=jnp.float32)


def inverse(tiles):
    lanes = tiles[0].shape[1]
    lane = lax.broadcasted_iota(jnp.int32, (8, lanes), 1)
    sub = lax.broadcasted_iota(jnp.int32, (8, lanes), 0)
    for k in range(0, lanes, 2):
        own, at = divmod(k, 8)
        first = lane == k
        second = lane == k + 1
        either = first | second
        col0 = [jnp.broadcast_to(t[:, k:k + 1], t.shape) for t in tiles]
        col1 = [jnp.broadcast_to(t[:, k + 1:k + 2], t.shape) for t in tiles]

        def spread(tile, row):
            return jnp.broadcast_to(tile[row:row + 1, :], tile.shape)

        a = spread(col0[own], at)
        b = spread(col1[own], at)
        d = spread(col1[own], at + 1)
        row0 = spread(tiles[own], at)
        row1 = spread(tiles[own], at + 1)
        row0 = jnp.where(first, 1.0, jnp.where(second, 0.0, row0))
        row1 = jnp.where(second, 1.0, jnp.where(first, 0.0, row1))
        scale = 1.0 / (a * d - b * b)
        t0 = (d * row0 - b * row1) * scale
        t1 = (a * row1 - b * row0) * scale
        out = []
        for i, tile in enumerate(tiles):
            new = jnp.where(either, 0.0, tile) - col0[i] * t0 - col1[i] * t1
            if i == own:
                new = jnp.where(sub == at, t0, jnp.where(sub == at + 1, t1, new))
            out.append(new)
        tiles = out
    return tiles


def factor_kernel(ridge, gram_ref, work_ref, inv_ref):
    size = gram_ref.shape[0]
    panels = size // PANEL
    diag = lax.broadcasted_iota(jnp.int32, (PANEL, size), 0)
    lane = lax.broadcasted_iota(jnp.int32, (PANEL, size), 1)

    @pl.loop(0, panels)
    def _(p):
        rows = pl.ds(pl.multiple_of(p * PANEL, PANEL), PANEL)
        work_ref[rows, :] = gram_ref[rows, :] + jnp.where(lane == diag + p * PANEL, ridge, 0.0)

    @pl.loop(0, panels)
    def _(p):
        start = pl.multiple_of(p * PANEL, PANEL)
        rows = pl.ds(start, PANEL)
        tiles = [work_ref[pl.ds(start + 8 * i, 8), rows] for i in range(PANEL // 8)]
        tiles = inverse(tiles)
        for i, tile in enumerate(tiles):
            inv_ref[pl.ds(start + 8 * i, 8), :] = tile
        right = lane >= start + PANEL
        scaled = jnp.where(right, dot(inv_ref[rows, :], work_ref[rows, :]), 0.0)
        work_ref[rows, :] = jnp.where(right, scaled, work_ref[rows, :])

        @pl.loop(p + 1, panels)
        def _(q):
            below = pl.ds(pl.multiple_of(q * PANEL, PANEL), PANEL)
            work_ref[below, :] = work_ref[below, :] - dot(work_ref[below, rows], scaled)


def solve_kernel(work_ref, inv_ref, corr_ref, out_ref):
    panels = work_ref.shape[0] // PANEL
    for p in range(panels):
        rows = slice(p * PANEL, (p + 1) * PANEL)
        here = corr_ref[rows, :]
        if p:
            here = here - dot(work_ref[rows, :p * PANEL], out_ref[:p * PANEL, :])
        out_ref[rows, :] = dot(inv_ref[rows, :], here)
    for p in range(panels - 2, -1, -1):
        rows = slice(p * PANEL, (p + 1) * PANEL)
        out_ref[rows, :] = out_ref[rows, :] - dot(
            work_ref[rows, (p + 1) * PANEL:], out_ref[(p + 1) * PANEL:, :]
        )


def body(frames, weights, phases, residual):
    rows_here = frames.shape[0]
    feature_count = weights.shape[1]
    preact = jnp.dot(
        lax.all_gather(frames, "tgt", axis=1, tiled=True),
        weights,
        preferred_element_type=jnp.float32,
    )
    feature = math.sqrt(2.0 / feature_count) * cosine(preact + phases[None, :])
    share = feature_count // lax.axis_size("tgt")
    mine = lax.dynamic_slice_in_dim(feature, lax.axis_index("tgt") * share, share, 1)
    gram = lax.psum(dot(mine.T, feature), "rows")
    corr, gram = lax.optimization_barrier((dot(feature.T, residual), gram))
    gram = lax.all_gather(gram, "tgt", axis=0, tiled=True)
    corr = lax.psum(corr, "rows")
    ridge = 0.1 * (rows_here * lax.axis_size("rows")) / feature_count
    work, inv = pl.pallas_call(
        functools.partial(factor_kernel, ridge),
        out_shape=(
            jax.ShapeDtypeStruct(gram.shape, jnp.float32),
            jax.ShapeDtypeStruct((feature_count, PANEL), jnp.float32),
        ),
        compiler_params=pltpu.CompilerParams(vmem_limit_bytes=LIMIT),
        cost_estimate=pl.CostEstimate(
            flops=8 * feature_count**3, bytes_accessed=8 * feature_count**2, transcendentals=0
        ),
        name="factor",
    )(gram)
    coefficients = pl.pallas_call(
        solve_kernel,
        out_shape=jax.ShapeDtypeStruct(corr.shape, jnp.float32),
        compiler_params=pltpu.CompilerParams(vmem_limit_bytes=LIMIT),
        name="solve",
    )(work, inv, corr)
    residual_next = residual - dot(feature, coefficients)
    return (residual_next, coefficients)


def solution(mesh):
    return jax.shard_map(
        body,
        mesh=mesh,
        in_specs=(P("rows", "tgt"), P(), P(), P("rows", "tgt")),
        out_specs=(P("rows", "tgt"), P(None, "tgt")),
        check_vma=False,
    )
```

```python
import functools
import math

import jax
import jax.numpy as jnp
from jax import lax
from jax.experimental import pallas as pl
from jax.experimental.pallas import tpu as pltpu
from jax.sharding import PartitionSpec as P

HIGHEST = lax.Precision.HIGHEST
PANEL = 128
LIMIT = 48 * 1024 * 1024
HALF = (
    0.9999999997778334,
    -0.49999999352232993 / 4,
    0.04166663603866973 / 16,
    -0.001388835871629621 / 64,
    2.4760028045058155e-05 / 256,
    -2.604918848612031e-07 / 1024,
)


def cosine(angle):
    turns = jnp.round(angle * (1.0 / (2.0 * math.pi)))
    rest = (angle - turns * 6.28125) - turns * (2.0 * math.pi - 6.28125)
    square = rest * rest
    half = jnp.full_like(square, HALF[-1])
    for term in HALF[-2::-1]:
        half = half * square + term
    return 2.0 * half * half - 1.0


def dot(a, b):
    return jnp.dot(a, b, precision=HIGHEST, preferred_element_type=jnp.float32)


def spread(tile, row):
    return jnp.broadcast_to(tile[row:row + 1, :], tile.shape)


def column(tile, lane):
    return jnp.broadcast_to(tile[:, lane:lane + 1], tile.shape)


def inverse(tiles):
    lanes = tiles[0].shape[1]
    lane = lax.broadcasted_iota(jnp.int32, (8, lanes), 1)
    sub = lax.broadcasted_iota(jnp.int32, (8, lanes), 0)
    for own in range(lanes // 8):
        base = 8 * own
        inside = (lane >= base) & (lane < base + 8)
        cols = [column(tiles[own], base + m) for m in range(8)]
        slab = jnp.where(inside, jnp.where(lane - base == sub, 1.0, 0.0), tiles[own])
        for j in range(0, 8, 2):
            a = spread(cols[j], j)
            b = spread(cols[j + 1], j)
            d = spread(cols[j + 1], j + 1)
            scale = 1.0 / (a * d - b * b)
            a, b, d = a * scale, b * scale, d * scale

            def step(v):
                v0, v1 = spread(v, j), spread(v, j + 1)
                t0 = d * v0 - b * v1
                t1 = a * v1 - b * v0
                new = v - cols[j] * t0 - cols[j + 1] * t1
                return jnp.where(sub == j, t0, jnp.where(sub == j + 1, t1, new))

            later = [step(c) for c in cols[j + 2:]]
            slab = step(slab)
            cols = cols[:j + 2] + later
        pivots = [spread(slab, m) for m in range(8)]
        out = []
        for i, tile in enumerate(tiles):
            if i == own:
                out.append(slab)
                continue
            new = jnp.where(inside, 0.0, tile)
            for m in range(8):
                new = new - column(tile, base + m) * pivots[m]
            out.append(new)
        tiles = out
    return tiles


def pack(pair, place, blocks):
    block = pair.shape[0] // 2
    upper, lower = pair[:block], pair[block:]
    lane = lax.broadcasted_iota(jnp.int32, (block, (blocks + 1) * block), 1)
    left = jnp.roll(upper, -place * block, axis=1)
    return jnp.where(
        lane < (blocks - place) * block,
        jnp.pad(left, ((0, 0), (0, block))),
        jnp.pad(lower, ((0, 0), (block, 0))),
    )


def factor_kernel(ridge, packed_ref, work_ref, inv_ref):
    size = work_ref.shape[0]
    panels = size // PANEL
    block = packed_ref.shape[1] - size
    blocks = size // block
    for place in range(blocks // 2):
        packed = slice(place * block, (place + 1) * block)
        other = blocks - 1 - place
        cut = (blocks - place) * block
        work_ref[packed, place * block:] = packed_ref[packed, :cut]
        work_ref[other * block:(other + 1) * block, other * block:] = packed_ref[packed, cut:]
    for i in range(blocks - 1):
        here = slice(i * block, (i + 1) * block)
        work_ref[(i + 1) * block:, here] = work_ref[here, (i + 1) * block:].T
    diag = lax.broadcasted_iota(jnp.int32, (PANEL, size), 0)
    lane = lax.broadcasted_iota(jnp.int32, (PANEL, size), 1)

    @pl.loop(0, panels)
    def _(p):
        rows = pl.ds(pl.multiple_of(p * PANEL, PANEL), PANEL)
        work_ref[rows, :] = work_ref[rows, :] + jnp.where(lane == diag + p * PANEL, ridge, 0.0)

    @pl.loop(0, panels)
    def _(p):
        start = pl.multiple_of(p * PANEL, PANEL)
        rows = pl.ds(start, PANEL)
        tiles = [work_ref[pl.ds(start + 8 * i, 8), rows] for i in range(PANEL // 8)]
        tiles = inverse(tiles)
        for i, tile in enumerate(tiles):
            inv_ref[pl.ds(start + 8 * i, 8), :] = tile
        right = lane >= start + PANEL
        scaled = jnp.where(right, dot(inv_ref[rows, :], work_ref[rows, :]), 0.0)
        work_ref[rows, :] = jnp.where(right, scaled, work_ref[rows, :])

        @pl.loop(p + 1, panels)
        def _(q):
            below = pl.ds(pl.multiple_of(q * PANEL, PANEL), PANEL)
            work_ref[below, :] = work_ref[below, :] - dot(work_ref[below, rows], scaled)


def solve_kernel(work_ref, inv_ref, corr_ref, out_ref):
    panels = work_ref.shape[0] // PANEL
    for p in range(panels):
        rows = slice(p * PANEL, (p + 1) * PANEL)
        here = corr_ref[rows, :]
        if p:
            here = here - dot(work_ref[rows, :p * PANEL], out_ref[:p * PANEL, :])
        out_ref[rows, :] = dot(inv_ref[rows, :], here)
    for p in range(panels - 2, -1, -1):
        rows = slice(p * PANEL, (p + 1) * PANEL)
        out_ref[rows, :] = out_ref[rows, :] - dot(
            work_ref[rows, (p + 1) * PANEL:], out_ref[(p + 1) * PANEL:, :]
        )


def body(frames, weights, phases, residual):
    rows_here = frames.shape[0]
    feature_count = weights.shape[1]
    preact = jnp.dot(
        lax.all_gather(frames, "tgt", axis=1, tiled=True),
        weights,
        preferred_element_type=jnp.float32,
    )
    feature = math.sqrt(2.0 / feature_count) * cosine(preact + phases[None, :])
    blocks = 2 * lax.axis_size("tgt")
    block = feature_count // blocks
    place = lax.axis_index("tgt")
    mine = jnp.concatenate(
        [
            lax.dynamic_slice_in_dim(feature, place * block, block, 1),
            lax.dynamic_slice_in_dim(feature, (blocks - 1 - place) * block, block, 1),
        ],
        axis=1,
    )
    gram = lax.psum(pack(dot(mine.T, feature), place, blocks), "rows")
    corr, gram = lax.optimization_barrier((dot(feature.T, residual), gram))
    gram = lax.all_gather(gram, "tgt", axis=0, tiled=True)
    corr = lax.psum(corr, "rows")
    ridge = 0.1 * (rows_here * lax.axis_size("rows")) / feature_count
    work, inv = pl.pallas_call(
        functools.partial(factor_kernel, ridge),
        out_shape=(
            jax.ShapeDtypeStruct((feature_count, feature_count), jnp.float32),
            jax.ShapeDtypeStruct((feature_count, PANEL), jnp.float32),
        ),
        compiler_params=pltpu.CompilerParams(vmem_limit_bytes=LIMIT),
        cost_estimate=pl.CostEstimate(
            flops=8 * feature_count**3, bytes_accessed=8 * feature_count**2, transcendentals=0
        ),
        name="factor",
    )(gram)
    coefficients = pl.pallas_call(
        solve_kernel,
        out_shape=jax.ShapeDtypeStruct(corr.shape, jnp.float32),
        compiler_params=pltpu.CompilerParams(vmem_limit_bytes=LIMIT),
        name="solve",
    )(work, inv, corr)
    residual_next = residual - jnp.dot(
        feature, coefficients, precision=lax.Precision.HIGH, preferred_element_type=jnp.float32
    )
    return (residual_next, coefficients)


def solution(mesh):
    return jax.shard_map(
        body,
        mesh=mesh,
        in_specs=(P("rows", "tgt"), P(), P(), P("rows", "tgt")),
        out_specs=(P("rows", "tgt"), P(None, "tgt")),
        check_vma=False,
    )
```

```python
import functools
import math

import jax
import jax.numpy as jnp
from jax import lax
from jax.experimental import pallas as pl
from jax.experimental.pallas import tpu as pltpu
from jax.sharding import PartitionSpec as P

HIGHEST = lax.Precision.HIGHEST
PANEL = 128
LIMIT = 48 * 1024 * 1024
HALF = (
    0.9999999997778334,
    -0.49999999352232993 / 4,
    0.04166663603866973 / 16,
    -0.001388835871629621 / 64,
    2.4760028045058155e-05 / 256,
    -2.604918848612031e-07 / 1024,
)


def cosine(angle):
    turns = jnp.round(angle * (1.0 / (2.0 * math.pi)))
    rest = (angle - turns * 6.28125) - turns * (2.0 * math.pi - 6.28125)
    square = rest * rest
    half = jnp.full_like(square, HALF[-1])
    for term in HALF[-2::-1]:
        half = half * square + term
    return 2.0 * half * half - 1.0


def dot(a, b):
    return jnp.dot(a, b, precision=HIGHEST, preferred_element_type=jnp.float32)


def spread(tile, row):
    return jnp.broadcast_to(tile[row:row + 1, :], tile.shape)


def column(tile, lane):
    return jnp.broadcast_to(tile[:, lane:lane + 1], tile.shape)


def inverse(tiles):
    lanes = tiles[0].shape[1]
    lane = lax.broadcasted_iota(jnp.int32, (8, lanes), 1)
    sub = lax.broadcasted_iota(jnp.int32, (8, lanes), 0)
    for own in range(lanes // 8):
        base = 8 * own
        inside = (lane >= base) & (lane < base + 8)
        cols = [column(tiles[own], base + m) for m in range(8)]
        slab = jnp.where(inside, jnp.where(lane - base == sub, 1.0, 0.0), tiles[own])
        for j in range(0, 8, 2):
            a = spread(cols[j], j)
            b = spread(cols[j + 1], j)
            d = spread(cols[j + 1], j + 1)
            scale = 1.0 / (a * d - b * b)
            a, b, d = a * scale, b * scale, d * scale

            def step(v):
                v0, v1 = spread(v, j), spread(v, j + 1)
                t0 = d * v0 - b * v1
                t1 = a * v1 - b * v0
                new = v - cols[j] * t0 - cols[j + 1] * t1
                return jnp.where(sub == j, t0, jnp.where(sub == j + 1, t1, new))

            later = [step(c) for c in cols[j + 2:]]
            slab = step(slab)
            cols = cols[:j + 2] + later
        pivots = [spread(slab, m) for m in range(8)]
        out = []
        for i, tile in enumerate(tiles):
            if i == own:
                out.append(slab)
                continue
            new = jnp.where(inside, 0.0, tile)
            for m in range(8):
                new = new - column(tile, base + m) * pivots[m]
            out.append(new)
        tiles = out
    return tiles


def pack(pair, place, blocks):
    block = pair.shape[0] // 2
    upper, lower = pair[:block], pair[block:]
    lane = lax.broadcasted_iota(jnp.int32, (block, (blocks + 1) * block), 1)
    left = jnp.roll(upper, -place * block, axis=1)
    return jnp.where(
        lane < (blocks - place) * block,
        jnp.pad(left, ((0, 0), (0, block))),
        jnp.pad(lower, ((0, 0), (block, 0))),
    )


def share_kernel(n_rows, n_tgt, part_ref, out_ref, land_ref, s1, r1, s2, r2, s3, r3, s4, r4):
    row, tgt = lax.axis_index("rows"), lax.axis_index("tgt")
    half = n_tgt // 2
    low = lax.rem(tgt, 2)
    far = [lax.rem(tgt + 2 * e, n_tgt) for e in range(1, half)]
    near = tgt + 1 - 2 * low

    def ahead(d):
        return lax.rem(row + d, n_rows)

    def behind(d):
        return lax.rem(row + n_rows - d, n_rows)

    peers = [(ahead(d), tgt) for d in range(1, n_rows)] + [(row, t) for t in far] + [(row, near)]
    barrier = pltpu.get_barrier_semaphore()
    for peer in peers:
        pl.semaphore_signal(barrier, inc=1, device_id=peer, device_id_type=pl.DeviceIdType.MESH)
    pl.semaphore_wait(barrier, len(peers))

    def send(src, dst, send_sem, recv_sem, peer):
        copy = pltpu.make_async_remote_copy(
            src_ref=src,
            dst_ref=dst,
            send_sem=send_sem,
            recv_sem=recv_sem,
            device_id=peer,
            device_id_type=pl.DeviceIdType.MESH,
        )
        copy.start()
        return copy

    scatter = [
        send(part_ref.at[ahead(d)], land_ref.at[d - 1], s1.at[d - 1], r1.at[d - 1], (ahead(d), tgt))
        for d in range(1, n_rows)
    ]
    total = part_ref[row]
    for d in range(1, n_rows):
        scatter[d - 1].wait_recv()
        total = total + land_ref[d - 1]
    out_ref[tgt, row] = total
    own = out_ref.at[tgt, row]
    gather = [
        send(own, own, s2.at[d - 1], r2.at[d - 1], (ahead(d), tgt)) for d in range(1, n_rows)
    ]
    across, beside = [], []
    for d in range(n_rows):
        if d:
            gather[d - 1].wait_recv()
        chunk = out_ref.at[tgt, behind(d)]
        across.append([
            send(chunk, chunk, s3.at[d, e], r3.at[d, e], (row, t)) for e, t in enumerate(far)
        ])
        beside.append([send(chunk, chunk, s4.at[d, 0], r4.at[d, 0], (row, near))])
    for d in range(n_rows):
        for e in range(1, half):
            across[d][e - 1].wait_recv()
            chunk = out_ref.at[lax.rem(tgt + n_tgt - 2 * e, n_tgt), behind(d)]
            beside[d].append(send(chunk, chunk, s4.at[d, e], r4.at[d, e], (row, near)))
    for d in range(n_rows):
        for copy in beside[d]:
            copy.wait_recv()
    for copy in scatter + gather + sum(across, []) + sum(beside, []):
        copy.wait_send()


def share(part):
    n_rows, n_tgt = lax.axis_size("rows"), lax.axis_size("tgt")
    chunk = part.shape[0] // n_rows
    sems = [
        pltpu.SemaphoreType.DMA(shape)
        for shape in (
            (n_rows - 1,),
            (n_rows - 1,),
            (n_rows - 1,),
            (n_rows - 1,),
            (n_rows, max(n_tgt // 2 - 1, 1)),
            (n_rows, max(n_tgt // 2 - 1, 1)),
            (n_rows, n_tgt // 2),
            (n_rows, n_tgt // 2),
        )
    ]
    out = pl.pallas_call(
        functools.partial(share_kernel, n_rows, n_tgt),
        out_shape=jax.ShapeDtypeStruct((n_tgt, n_rows, chunk, part.shape[1]), jnp.float32),
        in_specs=[pl.BlockSpec(memory_space=pltpu.VMEM)],
        out_specs=pl.BlockSpec(memory_space=pltpu.VMEM),
        scratch_shapes=[pltpu.VMEM((n_rows - 1, chunk, part.shape[1]), jnp.float32), *sems],
        compiler_params=pltpu.CompilerParams(
            collective_id=0, has_side_effects=True, vmem_limit_bytes=LIMIT
        ),
        name="share",
    )(part.reshape(n_rows, chunk, part.shape[1]))
    return out.reshape(n_tgt * part.shape[0], part.shape[1])


def factor_kernel(ridge, packed_ref, work_ref, inv_ref):
    size = work_ref.shape[0]
    panels = size // PANEL
    block = packed_ref.shape[1] - size
    blocks = size // block
    for place in range(blocks // 2):
        packed = slice(place * block, (place + 1) * block)
        other = blocks - 1 - place
        cut = (blocks - place) * block
        work_ref[packed, place * block:] = packed_ref[packed, :cut]
        work_ref[other * block:(other + 1) * block, other * block:] = packed_ref[packed, cut:]
    for i in range(blocks - 1):
        here = slice(i * block, (i + 1) * block)
        work_ref[(i + 1) * block:, here] = work_ref[here, (i + 1) * block:].T
    diag = lax.broadcasted_iota(jnp.int32, (PANEL, size), 0)
    lane = lax.broadcasted_iota(jnp.int32, (PANEL, size), 1)

    @pl.loop(0, panels)
    def _(p):
        rows = pl.ds(pl.multiple_of(p * PANEL, PANEL), PANEL)
        work_ref[rows, :] = work_ref[rows, :] + jnp.where(lane == diag + p * PANEL, ridge, 0.0)

    @pl.loop(0, panels)
    def _(p):
        start = pl.multiple_of(p * PANEL, PANEL)
        rows = pl.ds(start, PANEL)
        tiles = [work_ref[pl.ds(start + 8 * i, 8), rows] for i in range(PANEL // 8)]
        tiles = inverse(tiles)
        for i, tile in enumerate(tiles):
            inv_ref[pl.ds(start + 8 * i, 8), :] = tile
        right = lane >= start + PANEL
        scaled = jnp.where(right, dot(inv_ref[rows, :], work_ref[rows, :]), 0.0)
        work_ref[rows, :] = jnp.where(right, scaled, work_ref[rows, :])

        @pl.loop(p + 1, panels)
        def _(q):
            below = pl.ds(pl.multiple_of(q * PANEL, PANEL), PANEL)
            work_ref[below, :] = work_ref[below, :] - dot(work_ref[below, rows], scaled)


def solve_kernel(work_ref, inv_ref, corr_ref, out_ref):
    panels = work_ref.shape[0] // PANEL
    for p in range(panels):
        rows = slice(p * PANEL, (p + 1) * PANEL)
        here = corr_ref[rows, :]
        if p:
            here = here - dot(work_ref[rows, :p * PANEL], out_ref[:p * PANEL, :])
        out_ref[rows, :] = dot(inv_ref[rows, :], here)
    for p in range(panels - 2, -1, -1):
        rows = slice(p * PANEL, (p + 1) * PANEL)
        out_ref[rows, :] = out_ref[rows, :] - dot(
            work_ref[rows, (p + 1) * PANEL:], out_ref[(p + 1) * PANEL:, :]
        )


def body(frames, weights, phases, residual):
    rows_here = frames.shape[0]
    feature_count = weights.shape[1]
    preact = jnp.dot(
        lax.all_gather(frames, "tgt", axis=1, tiled=True),
        weights,
        preferred_element_type=jnp.float32,
    )
    feature = math.sqrt(2.0 / feature_count) * cosine(preact + phases[None, :])
    blocks = 2 * lax.axis_size("tgt")
    block = feature_count // blocks
    place = lax.axis_index("tgt")
    mine = jnp.concatenate(
        [
            lax.dynamic_slice_in_dim(feature, place * block, block, 1),
            lax.dynamic_slice_in_dim(feature, (blocks - 1 - place) * block, block, 1),
        ],
        axis=1,
    )
    part = pack(dot(mine.T, feature), place, blocks)
    corr, part = lax.optimization_barrier((dot(feature.T, residual), part))
    corr = lax.psum(corr, "rows")
    gram = share(part)
    ridge = 0.1 * (rows_here * lax.axis_size("rows")) / feature_count
    work, inv = pl.pallas_call(
        functools.partial(factor_kernel, ridge),
        out_shape=(
            jax.ShapeDtypeStruct((feature_count, feature_count), jnp.float32),
            jax.ShapeDtypeStruct((feature_count, PANEL), jnp.float32),
        ),
        compiler_params=pltpu.CompilerParams(vmem_limit_bytes=LIMIT),
        cost_estimate=pl.CostEstimate(
            flops=8 * feature_count**3, bytes_accessed=8 * feature_count**2, transcendentals=0
        ),
        name="factor",
    )(gram)
    coefficients = pl.pallas_call(
        solve_kernel,
        out_shape=jax.ShapeDtypeStruct(corr.shape, jnp.float32),
        compiler_params=pltpu.CompilerParams(vmem_limit_bytes=LIMIT),
        name="solve",
    )(work, inv, corr)
    residual_next = residual - jnp.dot(
        feature, coefficients, precision=lax.Precision.HIGH, preferred_element_type=jnp.float32
    )
    return (residual_next, coefficients)


def solution(mesh):
    return jax.shard_map(
        body,
        mesh=mesh,
        in_specs=(P("rows", "tgt"), P(), P(), P("rows", "tgt")),
        out_specs=(P("rows", "tgt"), P(None, "tgt")),
        check_vma=False,
    )
```
